32 devices in a mesh: depth: 2 (over core), lat: 16 (over z, y, x).
Axes of the slice: x: 2, y: 2, z: 4, core: 2. Of those that a mesh axis runs over, the one named last changes fastest.
Arguments:
- object_slices: float32 [2, 2, 4096, 2048], P('depth', None, 'lat'), may hold values from -1.1 to 1.1, as said below
- probe: float32 [2, 256, 256], replicated, may hold values from -6 to 6
- measured: float32 [64, 256, 256], P('lat'), may hold values from 0.2 to 3
- positions: int32 [64, 2], P('lat'), may hold values from 0 to 1792, as said below
- counts: int32 [16], P('lat'), may hold values from 1 to 4, 40 in all
Outputs:
- object_gradient: float32 [2, 2, 4096, 2048], P('depth', None, 'lat')
The draws below stay inside these ranges and needn't reach their ends.
Inputs may be any that keep to these rules, and one draw needn't show every extreme that they name: `object_slices`: each transmission value has modulus at most 1.1. `positions`: column 0 is a row offset within the slot's own tile, from 0 to 255; column 1 is a column offset from 0 to 1792; both ends are reached. `counts`: every tile uses at least one slot; some tile uses all 4.
All inputs are finite; a program needn't handle non-finite values. No bound on the sum of `counts` on one device may be relied on, other than what follows from the above.
Results may differ from the reference program's by a relative error of at most 0.0003.
Values sent between devices are 32-bit elements; how exact they have to be, the bound alone decides.
No kernel may reach another device: no remote copies, remote signals or barrier semaphores. Data moves between devices by JAX's collectives and lax.ppermute only.
A program may use at most 128 MiB of HBM per device.

```python
import math
import jax
import jax.numpy as jnp
import numpy as np
from jax import lax

PROBE = 256
TILE_H = 256
OBJ_W = 2048
POS_CAP = 4
SLICES = 2
ROWS = 4096
POSITIONS = 64
LIVE = 40
N_LAT = 16


def draw_object_slices(key, part):
    first, second = jax.random.split(jax.random.fold_in(key, 11))
    shape = (SLICES, ROWS, OBJ_W)
    amplitude = jax.random.uniform(first, shape, jnp.float32, 0.6, 1.1)
    phase = jax.random.uniform(second, shape, jnp.float32, -1.0, 1.0)
    return jnp.stack([amplitude * jnp.cos(phase), amplitude * jnp.sin(phase)], axis=1).astype(jnp.float32)


def draw_positions(key, part):
    first, second = jax.random.split(jax.random.fold_in(key, 23))
    row_offsets = jax.random.randint(first, (POSITIONS,), 0, TILE_H, dtype=jnp.int32)
    column_offsets = jax.random.randint(second, (POSITIONS,), 0, OBJ_W - PROBE + 1, dtype=jnp.int32)
    row_offsets = row_offsets.at[1].set(TILE_H - 1).at[2].set(0)
    column_offsets = column_offsets.at[0].set(OBJ_W - PROBE).at[3].set(0)
    return jnp.stack([row_offsets, column_offsets], axis=1).astype(jnp.int32)


def level_of(key, extent, shards, least, largest):
    loudness = 1.0
    for axis_at, shards_of in shards:
        draws = jax.random.uniform(jax.random.fold_in(jax.random.fold_in(key, 6), axis_at), (shards_of,), jnp.float32, least / len(shards), largest / len(shards))
        loudness = loudness * jnp.repeat(jnp.exp(draws), extent[axis_at] // shards_of).reshape((-1,) + (1,) * (len(extent) - 1 - axis_at))
    return loudness


def length_profile(number_of, total, reach, skew):
    loads = [(1 << 20) // math.isqrt(rank ** skew) + 1 for rank in range(2, number_of + 1)]
    spare, holding = total - reach - (number_of - 1), [1] * (number_of - 1)
    while spare > 0:
        free = [i for i in range(number_of - 1) if holding[i] < reach]
        mass, left = sum([loads[i] for i in free]), spare
        for i in free:
            extra = min(reach - holding[i], max(1, left * loads[i] // mass), spare)
            holding[i] = holding[i] + extra
            spare = spare - extra
    return np.array([reach] + holding)


def uneven_parts(stream_key, number_of, total, reach, slope):
    if number_of == 2:
        one = jax.random.randint(stream_key, (), max(1, total - reach), min(reach, total - 1) + 1)
        return jnp.stack([one, total - one])
    lengths = jnp.asarray(length_profile(number_of, total, reach, slope), jnp.int32)
    couples = (number_of - 1) // 2
    source_of, sink = lengths[1:1 + 2 * couples:2], lengths[2:2 + 2 * couples:2]
    room = jnp.minimum(source_of - 1, reach - sink)
    passed = jax.random.randint(jax.random.fold_in(stream_key, 1), (couples,), 0, 1 << 20) % (room + 1)
    lengths = lengths.at[1:1 + 2 * couples:2].set(source_of - passed).at[2:2 + 2 * couples:2].set(sink + passed)
    return lengths[jax.random.permutation(jax.random.fold_in(stream_key, 2), number_of)]


def gaussian(key, dims, scale, most, kind=jnp.bfloat16):
    result = jax.random.normal(key, dims, jnp.float32) * scale
    return jnp.minimum(jnp.maximum(result, -most), most).astype(kind)


def setup_inputs(seed: int = 0) -> dict:
    streams_of = jax.random.split(jax.random.key(seed), 6)
    object_slices = draw_object_slices(jax.random.fold_in(streams_of[5], 71), 0)
    probe = gaussian(streams_of[1], (2, PROBE, PROBE), 1.0, 6.0, jnp.float32)
    measured = jnp.clip(0.2 + 2.8 * jax.random.uniform(streams_of[2], (POSITIONS, PROBE, PROBE), jnp.float32) ** level_of(streams_of[2], (POSITIONS, PROBE, PROBE), ((0, 16),), -0.2, 0.2), 0.2, 3.0)
    positions = draw_positions(jax.random.fold_in(streams_of[5], 71), 0)
    counts = uneven_parts(streams_of[4], N_LAT, LIVE, POS_CAP, 2).astype(jnp.int32)
    return dict(object_slices=object_slices, probe=probe, measured=measured, positions=positions, counts=counts)


fresnel_strength = 8.0

def dft_tables(length):
    index = jnp.arange(length, dtype=jnp.int32)
    product = index[:, None] * index[None, :] % length
    angle = 2.0 * math.pi / length * product.astype(jnp.float32)
    scale = 1.0 / math.sqrt(length)
    return (jnp.cos(angle) * scale, jnp.sin(angle) * scale)

def kernel_tables(length):
    index = jnp.arange(length, dtype=jnp.int32)
    centred = (index - length * (index >= length // 2).astype(jnp.int32)).astype(jnp.float32) / length
    phase = math.pi * fresnel_strength * (centred[:, None] ** 2 + centred[None, :] ** 2)
    return (jnp.cos(phase), jnp.sin(phase))

def left_product(matrix, values):
    return jnp.einsum('jk,...kl->...jl', matrix, values, precision=lax.Precision.HIGHEST)

def right_product(values, matrix):
    return jnp.einsum('...jk,kl->...jl', values, matrix, precision=lax.Precision.HIGHEST)

def transform(values, tables, sign):
    cosine, sine = tables
    sine = sine * sign
    left_real = left_product(cosine, values[0]) - left_product(sine, values[1])
    left_imaginary = left_product(cosine, values[1]) + left_product(sine, values[0])
    out_real = right_product(left_real, cosine) - right_product(left_imaginary, sine)
    out_imaginary = right_product(left_imaginary, cosine) + right_product(left_real, sine)
    return jnp.stack([out_real, out_imaginary])

def complex_product(first, second):
    return jnp.stack([first[0] * second[0] - first[1] * second[1], first[0] * second[1] + first[1] * second[0]])

def conj_product(first, second):
    return jnp.stack([first[0] * second[0] + first[1] * second[1], first[0] * second[1] - first[1] * second[0]])

def propagate(values, tables, kernel, sign):
    spectrum = transform(values, tables, -1.0)
    turned = complex_product(spectrum, jnp.stack([kernel[0], sign * kernel[1]]))
    return transform(turned, tables, 1.0)

def reference(object_slices, probe, measured, positions, counts):
    tables = dft_tables(PROBE)
    kernel = kernel_tables(PROBE)
    offsets = jnp.arange(PROBE, dtype=jnp.int32)

    def one_position(index):
        device = index // POS_CAP
        slot_number = index % POS_CAP
        first_row = device * TILE_H + positions[index, 0]
        row_index = ((first_row + offsets) % ROWS).astype(jnp.int32)
        column_index = (positions[index, 1] + offsets).astype(jnp.int32)
        window = object_slices[:, :, row_index[:, None], column_index[None, :]]
        live = (slot_number < counts[device]).astype(jnp.float32)
        wave = probe
        inputs = []
        for layer in range(SLICES):
            inputs.append(wave)
            wave = propagate(complex_product(wave, window[layer]), tables, kernel, 1.0)
        far = transform(wave, tables, -1.0)
        factor = live * (1.0 - measured[index] / jnp.sqrt(far[0] * far[0] + far[1] * far[1] + 1.0))
        back = transform(far * factor, tables, 1.0)
        pieces = [None] * SLICES
        for layer in reversed(range(SLICES)):
            adjoint = propagate(back, tables, kernel, -1.0)
            pieces[layer] = conj_product(inputs[layer], adjoint)
            back = conj_product(window[layer], adjoint)
        return (jnp.stack(pieces), row_index, column_index)
    gradients, row_lists, column_lists = lax.map(one_position, jnp.arange(POSITIONS, dtype=jnp.int32))

    def accumulate(total, item):
        piece, row_index, column_index = item
        return (total.at[:, :, row_index[:, None], column_index[None, :]].add(piece), None)
    total, unused = lax.scan(accumulate, jnp.zeros(object_slices.shape, jnp.float32), (gradients, row_lists, column_lists))
    return total
```

```python
import functools
import math

import jax
import jax.numpy as jnp
import numpy as np
from jax import lax
from jax.experimental import pallas as pl
from jax.experimental.pallas import tpu as pltpu
from jax.sharding import PartitionSpec as P

fresnel_strength = 8.0
STEP = 32
VMEM = pl.BlockSpec(memory_space=pltpu.VMEM)
SMEM = pl.BlockSpec(memory_space=pltpu.SMEM)
ANY = pl.BlockSpec(memory_space=pl.ANY)


def shift(value, axis, by):
    length = lax.axis_size(axis)
    return lax.ppermute(value, axis, [(i, (i + by) % length) for i in range(length)])


def tables_of(length):
    index = np.arange(length)
    angle = 2.0 * np.pi / length * (index[:, None] * index[None, :] % length)
    matrix = (np.cos(angle) - 1j * np.sin(angle)) / math.sqrt(length)
    centred = (index - length * (index >= length // 2)) / length
    turn = np.exp(1j * np.pi * fresnel_strength * centred**2)
    propagator = np.conj(matrix) @ (turn[:, None] * matrix)
    parts = []
    for table in (propagator, matrix):
        for part in (table.real, table.imag, -table.imag):
            high = part.astype(jnp.bfloat16)
            low = (part - high.astype(np.float64)).astype(jnp.bfloat16)
            parts += [high, low]
    return np.stack(parts)


def split(value):
    high = value.astype(jnp.bfloat16)
    return high, (value - high.astype(jnp.float32)).astype(jnp.bfloat16)


def dot(first, second):
    return jnp.dot(first, second, preferred_element_type=jnp.float32)


def two_sided(values, tables, which):
    width = values[0][0].shape[0]
    rh, rl, ih, il, nh, nl = [tables[6 * which + i] for i in range(6)]
    real = jnp.concatenate([v[0] for v in values], axis=1)
    imaginary = jnp.concatenate([v[1] for v in values], axis=1)
    (rh_x, rl_x), (ih_x, il_x) = split(real), split(imaginary)
    highs = jnp.concatenate([rh_x, ih_x], axis=0)
    both = jnp.concatenate([rh_x, ih_x, rl_x, il_x], axis=0)
    left = []
    for high, low in (((rh, nh), (rl, nl)), ((ih, rh), (il, rl))):
        left.append(
            dot(jnp.concatenate(high + high, axis=1), both) + dot(jnp.concatenate(low, axis=1), highs)
        )
    real, imaginary = [
        jnp.concatenate([v[:, i * width : (i + 1) * width] for i in range(len(values))], axis=0)
        for v in left
    ]
    (rh_x, rl_x), (ih_x, il_x) = split(real), split(imaginary)
    highs = jnp.concatenate([rh_x, ih_x], axis=1)
    both = jnp.concatenate([rh_x, ih_x, rl_x, il_x], axis=1)
    right = []
    for high, low in (((rh, nh), (rl, nl)), ((ih, rh), (il, rl))):
        right.append(
            dot(both, jnp.concatenate(high + high, axis=0)) + dot(highs, jnp.concatenate(low, axis=0))
        )
    return [tuple(v[i * width : (i + 1) * width] for v in right) for i in range(len(values))]


def product(first, second):
    return (
        first[0] * second[0] - first[1] * second[1],
        first[0] * second[1] + first[1] * second[0],
    )


def conj_product(first, second):
    return (
        first[0] * second[0] + first[1] * second[1],
        first[0] * second[1] - first[1] * second[0],
    )


def conj(value):
    return value[0], -value[1]


def places(meta, tile, slots, width, columns):
    found, start = [], 0
    for slot in range(slots):
        live = slot < meta[tile, 2 * slots]
        row = jnp.where(live, meta[tile, 2 * slot], 0)
        column = meta[tile, 2 * slot + 1]
        block = jnp.minimum(column // width, columns // width - 2)
        rows = (row + 7) // 8 * 8
        found.append((live, row, block, column - block * width, start, rows))
        start = start + rows
    return found


def for_rows(first, last, body):
    whole = (last - first) // STEP

    def big(i, carry):
        body(pl.multiple_of(first + i * STEP, 8), STEP)
        return carry

    def small(i, carry):
        body(pl.multiple_of(first + whole * STEP + i * 8, 8), 8)
        return carry

    lax.fori_loop(0, whole, big, 0)
    lax.fori_loop(0, (last - first - whole * STEP) // 8, small, 0)


def row_ids(row, size, width):
    return row + lax.broadcasted_iota(jnp.int32, (size, width), 0)


def column_ids(size, width):
    return lax.broadcasted_iota(jnp.int32, (size, width), 1)


def fetch(objects, buffers, semaphores, slot, place, width):
    return pltpu.make_async_copy(
        objects.at[0, :, :, pl.ds(pl.multiple_of(place[2] * width, width), 2 * width)],
        buffers.at[slot],
        semaphores.at[slot],
    )


def chosen(buffer, component, row, size, offset, width):
    here = buffer[component, pl.ds(row, size), 0:width]
    after = buffer[component, pl.ds(row, size), width : 2 * width]
    return jnp.where(column_ids(size, width) >= offset, here, after)


def pack_kernel(slots, width, columns, meta, objects, packed, buffers, semaphores):
    tiles = lax.axis_size("lat")
    tile = lax.rem(lax.axis_index("lat") + tiles - 1, tiles)
    spots = places(meta, tile, slots, width, columns)
    copies = [fetch(objects, buffers, semaphores, s, spots[s], width) for s in range(slots)]
    for copy in copies:
        copy.start()
    for slot in range(slots):
        copies[slot].wait()
        offset, start, rows = spots[slot][3:]

        def body(row, size):
            to = pl.ds(pl.multiple_of(start + row, 8), size)
            for component in range(2):
                packed[to, component * width : (component + 1) * width] = chosen(
                    buffers.at[slot], component, row, size, offset, width
                )

        for_rows(0, rows, body)


def local_kernel(slots, width, columns, meta, objects, own, given, buffers, semaphores):
    tile, depth = lax.axis_index("lat"), lax.axis_index("depth")
    spots = places(meta, tile, slots, width, columns)
    copies = [fetch(objects, buffers, semaphores, s, spots[s], width) for s in range(slots)]
    for copy in copies:
        copy.start()
    for slot in range(slots):
        copies[slot].wait()
        offset = spots[slot][3]

        def cut(target):
            def body(row, size):
                for component in range(2):
                    target[
                        slot // 2, pl.ds(row, size), component * width : (component + 1) * width
                    ] = chosen(buffers.at[slot], component, row, size, offset, width)

            for_rows(0, width, body)

        pl.when(depth == slot % 2)(functools.partial(cut, own))
        pl.when(depth != slot % 2)(functools.partial(cut, given))


def wave_kernel(
    slots, width, columns, meta, probe, measured, own, got, halo, halo_other, tables, kept, given, windows
):
    tile, depth = lax.axis_index("lat"), lax.axis_index("depth")
    spots = places(meta, tile, slots, width, columns)
    pairs = slots // 2
    mine = []
    for i in range(pairs):
        first, second = spots[2 * i], spots[2 * i + 1]
        mine.append([jnp.where(depth == 0, a, b) for a, b in zip(first, second)])
    for i in range(pairs):
        row_offset, start, rows = mine[i][1], mine[i][4], mine[i][5]
        for which, (near, far) in enumerate(((own, halo), (got, halo_other))):
            windows[which, i] = near[i]

            def body(row, size):
                to = pl.ds(row, size)
                there = far[pl.ds(pl.multiple_of(start + row, 8), size), :]
                windows[which, i, to, :] = jnp.where(
                    row_ids(row, size, 2 * width) < row_offset, there, windows[which, i, to, :]
                )

            for_rows(0, rows, body)

    def slab(layer, i):
        which = jnp.where(depth == layer, 0, 1)
        return windows[which, i, :, 0:width], windows[which, i, :, width : 2 * width]

    probes, first, second, levels = [], [], [], []
    for i in range(pairs):
        turn = lax.rem(mine[i][3], width)
        rolled = []
        for component in range(2):
            rolled.append(pltpu.roll(pltpu.roll(probe[component], mine[i][1], 0), turn, 1))
        probes.append(tuple(rolled))
        first.append(slab(0, i))
        second.append(slab(1, i))
    inner = two_sided([product(p, o) for p, o in zip(probes, first)], tables, 0)
    spectrum = two_sided([product(p, o) for p, o in zip(inner, second)], tables, 1)
    turned = []
    for i in range(pairs):
        real, imaginary = spectrum[i]
        amplitude = measured[2 * i + depth]
        live = jnp.where(mine[i][0], 1.0, 0.0)
        factor = live * (1.0 - amplitude * lax.rsqrt(real * real + imaginary * imaginary + 1.0))
        turned.append((real * factor, -imaginary * factor))
    adjoint = [conj(v) for v in two_sided(turned, tables, 1)]
    grad_second = [conj_product(p, a) for p, a in zip(inner, adjoint)]
    back = [conj(conj_product(o, a)) for o, a in zip(second, adjoint)]
    adjoint = [conj(v) for v in two_sided(back, tables, 0)]
    grad_first = [conj_product(p, a) for p, a in zip(probes, adjoint)]
    for i in range(pairs):
        for component in range(2):
            lanes = slice(component * width, (component + 1) * width)
            one, two = grad_first[i][component], grad_second[i][component]
            kept[i, :, lanes] = jnp.where(depth == 0, one, two)
            given[i, :, lanes] = jnp.where(depth == 0, two, one)


def spill_kernel(slots, width, columns, meta, kept, got, packed):
    tile, depth = lax.axis_index("lat"), lax.axis_index("depth")
    spots = places(meta, tile, slots, width, columns)
    for slot in range(slots):
        row_offset, start, rows = spots[slot][1], spots[slot][4], spots[slot][5]

        def put(source):
            def body(row, size):
                packed[pl.ds(pl.multiple_of(start + row, 8), size), :] = jnp.where(
                    row_ids(row, size, 2 * width) < row_offset,
                    source[slot // 2, pl.ds(row, size), :],
                    0.0,
                )

            for_rows(0, rows, body)

        pl.when(depth == slot % 2)(functools.partial(put, kept))
        pl.when(depth != slot % 2)(functools.partial(put, got))


def add_window(total, values, row, size, place, width):
    block, offset = place[2], place[3]
    columns = column_ids(size, width)
    for component in range(2):
        value = values[component]
        for half, mask in ((0, columns >= offset), (1, columns < offset)):
            to = pl.ds(pl.multiple_of((block + half) * width, width), width)
            total[component, pl.ds(row, size), to] += jnp.where(mask, value, 0.0)


def local_sum_kernel(slots, width, columns, meta, kept, got, total):
    tile, depth = lax.axis_index("lat"), lax.axis_index("depth")
    spots = places(meta, tile, slots, width, columns)
    total[...] = jnp.zeros_like(total)
    for slot in range(slots):
        live, row_offset = spots[slot][:2]

        def put(source):
            def body(row, size):
                keep = row_ids(row, size, width) >= row_offset
                values = []
                for component in range(2):
                    value = source[
                        slot // 2, pl.ds(row, size), component * width : (component + 1) * width
                    ]
                    values.append(jnp.where(keep, value, 0.0))
                add_window(total, values, row, size, spots[slot], width)

            for_rows(row_offset // 8 * 8, width, body)

        pl.when(live & (depth == slot % 2))(functools.partial(put, kept))
        pl.when(live & (depth != slot % 2))(functools.partial(put, got))


def last_kernel(slots, width, columns, meta, near, packed, result, total, semaphore):
    tiles = lax.axis_size("lat")
    tile = lax.rem(lax.axis_index("lat") + tiles - 1, tiles)
    spots = places(meta, tile, slots, width, columns)
    total[...] = near[...]
    for slot in range(slots):
        start, rows = spots[slot][4:]

        def body(row, size):
            values = []
            for component in range(2):
                values.append(
                    packed[
                        pl.ds(pl.multiple_of(start + row, 8), size),
                        component * width : (component + 1) * width,
                    ]
                )
            add_window(total, values, row, size, spots[slot], width)

        for_rows(0, rows, body)
    copy = pltpu.make_async_copy(total, result.at[0], semaphore)
    copy.start()
    copy.wait()


def call(kernel, inputs, outputs, specs, out_specs, scratch, flops, name):
    moved = sum(x.size * x.dtype.itemsize for x in list(inputs) + list(outputs))
    return pl.pallas_call(
        kernel,
        out_shape=outputs,
        in_specs=specs,
        out_specs=out_specs,
        scratch_shapes=scratch,
        compiler_params=pltpu.CompilerParams(vmem_limit_bytes=40 << 20),
        cost_estimate=pl.CostEstimate(flops=flops, bytes_accessed=moved, transcendentals=0),
        name=name,
    )(*inputs)


def run(rows, objects, probe, measured, meta, tables):
    slots, width = measured.shape[:2]
    columns = objects.shape[3]
    sizes = (slots, width, columns)
    f32 = jnp.float32
    packed_shape = jax.ShapeDtypeStruct((rows, 2 * width), f32)
    half_shape = jax.ShapeDtypeStruct((slots // 2, width, 2 * width), f32)
    tile_shape = jax.ShapeDtypeStruct(objects.shape[1:], f32)
    staging = [
        pltpu.VMEM((slots, 2, width, 2 * width), f32),
        pltpu.SemaphoreType.DMA((slots,)),
    ]
    packed = call(
        functools.partial(pack_kernel, *sizes), (meta, objects), [packed_shape],
        [SMEM, ANY], [VMEM], staging, 0, "pack",
    )[0]
    halo = shift(packed, "lat", -1)
    own, given = call(
        functools.partial(local_kernel, *sizes), (meta, objects), [half_shape] * 2,
        [SMEM, ANY], [VMEM] * 2, staging, 0, "local",
    )
    got = shift(given, "depth", 1)
    halo_other = shift(halo, "depth", 1)
    kept, given = call(
        functools.partial(wave_kernel, *sizes),
        (meta, probe, measured, own, got, halo, halo_other, tables),
        [half_shape] * 2,
        [SMEM] + [VMEM] * 7,
        [VMEM] * 2,
        [pltpu.VMEM((2, slots // 2, width, 2 * width), f32)],
        slots // 2 * 4 * 2 * 12 * 2 * width**3,
        "waves",
    )
    got = shift(given, "depth", 1)
    packed = call(
        functools.partial(spill_kernel, *sizes), (meta, kept, got), [packed_shape],
        [SMEM] + [VMEM] * 2, [VMEM], [], 0, "spill",
    )[0]
    spill = shift(packed, "lat", 1)
    near = call(
        functools.partial(local_sum_kernel, *sizes), (meta, kept, got), [tile_shape],
        [SMEM] + [VMEM] * 2, [VMEM], [], 0, "near",
    )[0]
    return call(
        functools.partial(last_kernel, *sizes), (meta, near, spill),
        [jax.ShapeDtypeStruct(objects.shape, f32)],
        [SMEM] + [VMEM] * 2, [ANY],
        [pltpu.VMEM(objects.shape[1:], f32), pltpu.SemaphoreType.DMA], 0, "last",
    )[0]


def shards(objects, probe, measured, positions, counts):
    slots, width = measured.shape[:2]
    tiles = lax.axis_size("lat")
    tables = jnp.asarray(tables_of(width))
    live = jnp.arange(slots, dtype=jnp.int32) < counts[0]
    packed_rows = jnp.sum(jnp.where(live, (positions[:, 0] + 7) // 8 * 8, 0), dtype=jnp.int32)
    line = jnp.concatenate([positions.reshape(-1), counts, packed_rows[None]])
    line = jnp.pad(line, (0, 128 - line.shape[0]))
    meta = lax.all_to_all(jnp.broadcast_to(line, (tiles, 128)), "lat", 0, 0, tiled=True)
    most = jnp.max(meta[:, 2 * slots + 1])
    full = slots * width
    steps = [full * i // 16 for i in range(4, 17)]
    which = jnp.sum(jnp.array(steps[:-1], jnp.int32) < most, dtype=jnp.int32)
    return lax.switch(
        which,
        [functools.partial(run, rows) for rows in steps],
        objects, probe, measured, meta, tables,
    )


def solution(mesh):
    return jax.shard_map(
        shards,
        mesh=mesh,
        in_specs=(
            P("depth", None, "lat", None),
            P(),
            P("lat", None, None),
            P("lat", None),
            P("lat"),
        ),
        out_specs=P("depth", None, "lat", None),
        check_vma=False,
    )
```

```python
import functools
import math

import jax
import jax.numpy as jnp
import numpy as np
from jax import lax
from jax.experimental import pallas as pl
from jax.experimental.pallas import tpu as pltpu
from jax.sharding import PartitionSpec as P

fresnel_strength = 8.0
STEP = 32
VMEM = pl.BlockSpec(memory_space=pltpu.VMEM)
SMEM = pl.BlockSpec(memory_space=pltpu.SMEM)
ANY = pl.BlockSpec(memory_space=pl.ANY)


def shift(value, axis, by):
    length = lax.axis_size(axis)
    return lax.ppermute(value, axis, [(i, (i + by) % length) for i in range(length)])


def tables_of(length):
    index = np.arange(length)
    angle = 2.0 * np.pi / length * (index[:, None] * index[None, :] % length)
    matrix = (np.cos(angle) - 1j * np.sin(angle)) / math.sqrt(length)
    centred = (index - length * (index >= length // 2)) / length
    turn = np.exp(1j * np.pi * fresnel_strength * centred**2)
    propagator = np.conj(matrix) @ (turn[:, None] * matrix)
    parts = []
    for table in (propagator, matrix):
        for part in (table.real, table.imag, -table.imag):
            high = part.astype(jnp.bfloat16)
            low = (part - high.astype(np.float64)).astype(jnp.bfloat16)
            parts += [high, low]
    return np.stack(parts)


def split(value):
    high = value.astype(jnp.bfloat16)
    return high, (value - high.astype(jnp.float32)).astype(jnp.bfloat16)


def dot(first, second):
    return jnp.dot(first, second, preferred_element_type=jnp.float32)


def two_sided(values, tables, which):
    width = values[0][0].shape[0]
    rh, rl, ih, il, nh, nl = [tables[6 * which + i] for i in range(6)]
    real = jnp.concatenate([v[0] for v in values], axis=1)
    imaginary = jnp.concatenate([v[1] for v in values], axis=1)
    (rh_x, rl_x), (ih_x, il_x) = split(real), split(imaginary)
    highs = jnp.concatenate([rh_x, ih_x], axis=0)
    both = jnp.concatenate([rh_x, ih_x, rl_x, il_x], axis=0)
    left = []
    for high, low in (((rh, nh), (rl, nl)), ((ih, rh), (il, rl))):
        left.append(
            dot(jnp.concatenate(high + high, axis=1), both) + dot(jnp.concatenate(low, axis=1), highs)
        )
    real, imaginary = [
        jnp.concatenate([v[:, i * width : (i + 1) * width] for i in range(len(values))], axis=0)
        for v in left
    ]
    (rh_x, rl_x), (ih_x, il_x) = split(real), split(imaginary)
    highs = jnp.concatenate([rh_x, ih_x], axis=1)
    both = jnp.concatenate([rh_x, ih_x, rl_x, il_x], axis=1)
    right = []
    for high, low in (((rh, nh), (rl, nl)), ((ih, rh), (il, rl))):
        right.append(
            dot(both, jnp.concatenate(high + high, axis=0)) + dot(highs, jnp.concatenate(low, axis=0))
        )
    return [tuple(v[i * width : (i + 1) * width] for v in right) for i in range(len(values))]


def product(first, second):
    return (
        first[0] * second[0] - first[1] * second[1],
        first[0] * second[1] + first[1] * second[0],
    )


def conj_product(first, second):
    return (
        first[0] * second[0] + first[1] * second[1],
        first[0] * second[1] - first[1] * second[0],
    )


def conj(value):
    return value[0], -value[1]


def bounds(slots, width):
    limit = width * 5 // 4
    up = 0
    for moved in range(1, slots):
        least = 8 * -(-(limit + 8) // (8 * (slots - moved + 1)))
        up = max(up, moved * (width - least + 8))
    return limit, up


def survey(positions, counts, slots, width, columns):
    limit = bounds(slots, width)[0]
    lives = [slot < counts[0] for slot in range(slots)]
    offsets = [positions[slot, 0] for slot in range(slots)]
    sizes = [jnp.where(v, (r + 7) // 8 * 8, 0) for v, r in zip(lives, offsets)]
    found = []
    stays = moves = down = up = jnp.int32(0)
    for slot in range(slots):
        total = sizes[slot]
        for other in range(slots):
            if other != slot:
                less = sizes[other] < sizes[slot]
                before = less | (sizes[other] == sizes[slot]) if other < slot else less
                total = total + jnp.where(before, sizes[other], 0)
        move = lives[slot] & (total > limit)
        stay = lives[slot] & jnp.logical_not(total > limit)
        column = positions[slot, 1]
        block = jnp.minimum(column // width, columns // width - 2)
        first = offsets[slot] // 8 * 8
        found.append(
            dict(
                row=offsets[slot], block=block, offset=column - block * width, stay=stay, move=move,
                stays=stays, moves=moves, down=down, up=up, size=sizes[slot], first=first,
            )
        )
        stays = stays + stay.astype(jnp.int32)
        moves = moves + move.astype(jnp.int32)
        down = down + jnp.where(stay, sizes[slot], 0)
        up = up + jnp.where(move, width - first, 0)
    return found, stays, moves


def entries(here, before):
    spots, _, _ = here
    spots_before, _, moves = before
    listed = [(s["move"], True, s["moves"], i, s) for i, s in enumerate(spots_before)]
    listed += [(s["stay"], False, moves + s["stays"], i, s) for i, s in enumerate(spots)]
    return listed


def for_rows(first, last, body):
    whole = (last - first) // STEP

    def big(i, carry):
        body(pl.multiple_of(first + i * STEP, 8), STEP)
        return carry

    def small(i, carry):
        body(pl.multiple_of(first + whole * STEP + i * 8, 8), 8)
        return carry

    lax.fori_loop(0, whole, big, 0)
    lax.fori_loop(0, (last - first - whole * STEP) // 8, small, 0)


def row_ids(row, size, width):
    return row + lax.broadcasted_iota(jnp.int32, (size, width), 0)


def column_ids(size, width):
    return lax.broadcasted_iota(jnp.int32, (size, width), 1)


def window_rows(objects, component, row, size, spot, width):
    block = spot["block"]
    here = objects[0, component, pl.ds(row, size), pl.ds(pl.multiple_of(block * width, width), width)]
    after = objects[0, component, pl.ds(row, size), pl.ds(pl.multiple_of((block + 1) * width, width), width)]
    return jnp.where(column_ids(size, width) >= spot["offset"], here, after)


def up_kernel(slots, width, columns, positions, counts, objects, measured, packed, levels, semaphores):
    depth = lax.axis_index("depth")
    spots, _, _ = survey(positions, counts, slots, width, columns)
    copies = []
    for i in range(slots // 2):
        chosen = jnp.int32(0)
        for slot, spot in enumerate(spots):
            chosen = jnp.where(spot["move"] & (spot["moves"] == 2 * i + depth), slot, chosen)
        copies.append(pltpu.make_async_copy(measured.at[chosen], levels.at[i], semaphores.at[i]))
        copies[i].start()
    for spot in spots:
        first, start = spot["first"], spot["up"]

        def body(row, size):
            to = pl.ds(pl.multiple_of(start + row - first, 8), size)
            for component in range(2):
                packed[to, component * width : (component + 1) * width] = window_rows(
                    objects, component, row, size, spot, width
                )

        pl.when(spot["move"])(functools.partial(for_rows, first, width, body))
    for copy in copies:
        copy.wait()


def down_kernel(slots, width, columns, positions, counts, objects, packed):
    spots, _, _ = survey(positions, counts, slots, width, columns)
    for spot in spots:
        start = spot["down"]

        def body(row, size):
            to = pl.ds(pl.multiple_of(start + row, 8), size)
            for component in range(2):
                packed[to, component * width : (component + 1) * width] = window_rows(
                    objects, component, row, size, spot, width
                )

        pl.when(spot["stay"])(functools.partial(for_rows, 0, spot["size"], body))


def local_kernel(slots, width, columns, positions, counts, positions_before, counts_before, objects, own, given):
    depth = lax.axis_index("depth")
    here = survey(positions, counts, slots, width, columns)
    before = survey(positions_before, counts_before, slots, width, columns)
    for active, moved, rank, _, spot in entries(here, before):
        first = 0 if moved else spot["first"]
        last = spot["size"] if moved else width

        def cut(target):
            def body(row, size):
                for component in range(2):
                    target[
                        rank // 2, pl.ds(row, size), component * width : (component + 1) * width
                    ] = window_rows(objects, component, row, size, spot, width)

            for_rows(first, last, body)

        pl.when(active & (rank % 2 == depth))(functools.partial(cut, own))
        pl.when(active & (rank % 2 != depth))(functools.partial(cut, given))


def wave_kernel(
    slots, width, columns, positions, counts, positions_before, counts_before, probe, measured, levels,
    own, got, down, down_other, up, up_other, tables, kept, given, windows, amplitudes, turns,
):
    depth = lax.axis_index("depth")
    here = survey(positions, counts, slots, width, columns)
    before = survey(positions_before, counts_before, slots, width, columns)
    for active, moved, rank, slot, spot in entries(here, before):

        @pl.when(active & (rank % 2 == depth))
        def _():
            at = rank // 2
            turns[at, 0] = spot["row"]
            turns[at, 1] = lax.rem(spot["offset"], width)
            amplitudes[at] = levels[at] if moved else measured[slot]
            middle = spot["size"] if moved else spot["first"]
            start = spot["up"] - spot["first"] if moved else spot["down"]
            far_first, far_last = (spot["first"], width) if moved else (0, spot["size"])
            near_first, near_last = (0, middle) if moved else (middle, width)
            for which, (near, far) in enumerate(((own, up if moved else down), (got, up_other if moved else down_other))):

                def copy(row, size):
                    windows[which, at, pl.ds(row, size), :] = near[at, pl.ds(row, size), :]

                def patch(row, size):
                    to = pl.ds(row, size)
                    there = far[pl.ds(pl.multiple_of(start + row, 8), size), :]
                    rows = row_ids(row, size, 2 * width)
                    mask = rows >= spot["row"] if moved else rows < spot["row"]
                    windows[which, at, to, :] = jnp.where(mask, there, windows[which, at, to, :])

                for_rows(near_first, near_last, copy)
                for_rows(far_first, far_last, patch)

    def slab(layer, at):
        which = jnp.where(depth == layer, 0, 1)
        return windows[which, at, :, 0:width], windows[which, at, :, width : 2 * width]

    def work(ats):
        probes, first, second = [], [], []
        for at in ats:
            rolled = []
            for component in range(2):
                rolled.append(pltpu.roll(pltpu.roll(probe[component], turns[at, 0], 0), turns[at, 1], 1))
            probes.append(tuple(rolled))
            first.append(slab(0, at))
            second.append(slab(1, at))
        inner = two_sided([product(p, o) for p, o in zip(probes, first)], tables, 0)
        spectrum = two_sided([product(p, o) for p, o in zip(inner, second)], tables, 1)
        turned = []
        for (real, imaginary), at in zip(spectrum, ats):
            factor = 1.0 - amplitudes[at] * lax.rsqrt(real * real + imaginary * imaginary + 1.0)
            turned.append((real * factor, -imaginary * factor))
        adjoint = [conj(v) for v in two_sided(turned, tables, 1)]
        grad_second = [conj_product(p, a) for p, a in zip(inner, adjoint)]
        back = [conj(conj_product(o, a)) for o, a in zip(second, adjoint)]
        adjoint = [conj(v) for v in two_sided(back, tables, 0)]
        grad_first = [conj_product(p, a) for p, a in zip(probes, adjoint)]
        for i, at in enumerate(ats):
            for component in range(2):
                lanes = slice(component * width, (component + 1) * width)
                one, two = grad_first[i][component], grad_second[i][component]
                kept[at, :, lanes] = jnp.where(depth == 0, one, two)
                given[at, :, lanes] = jnp.where(depth == 0, two, one)

    held = (here[1] + before[2] + 1 - depth) // 2

    def pair(i, carry):
        work([2 * i, 2 * i + 1])
        return carry

    lax.fori_loop(0, held // 2, pair, 0)

    @pl.when(held % 2 == 1)
    def _():
        work([held - 1])


def spill_kernel(
    slots, width, columns, positions, counts, positions_before, counts_before, kept, got, down, up
):
    depth = lax.axis_index("depth")
    here = survey(positions, counts, slots, width, columns)
    before = survey(positions_before, counts_before, slots, width, columns)
    for active, moved, rank, _, spot in entries(here, before):
        start = spot["up"] - spot["first"] if moved else spot["down"]
        first, last = (spot["first"], width) if moved else (0, spot["size"])
        packed = up if moved else down

        def put(source):
            def body(row, size):
                rows = row_ids(row, size, 2 * width)
                mask = rows >= spot["row"] if moved else rows < spot["row"]
                packed[pl.ds(pl.multiple_of(start + row, 8), size), :] = jnp.where(
                    mask, source[rank // 2, pl.ds(row, size), :], 0.0
                )

            for_rows(first, last, body)

        pl.when(active & (rank % 2 == depth))(functools.partial(put, kept))
        pl.when(active & (rank % 2 != depth))(functools.partial(put, got))


def add_window(total, values, row, size, spot, width):
    block, offset = spot["block"], spot["offset"]
    columns = column_ids(size, width)
    for component in range(2):
        value = values[component]
        for half, mask in ((0, columns >= offset), (1, columns < offset)):
            to = pl.ds(pl.multiple_of((block + half) * width, width), width)
            total[component, pl.ds(row, size), to] += jnp.where(mask, value, 0.0)


def near_kernel(
    slots, width, columns, positions, counts, positions_before, counts_before, kept, got, total
):
    depth = lax.axis_index("depth")
    here = survey(positions, counts, slots, width, columns)
    before = survey(positions_before, counts_before, slots, width, columns)
    total[...] = jnp.zeros_like(total)
    for active, moved, rank, _, spot in entries(here, before):
        first, last = (0, spot["size"]) if moved else (spot["first"], width)

        def put(source):
            def body(row, size):
                rows = row_ids(row, size, width)
                keep = rows < spot["row"] if moved else rows >= spot["row"]
                values = []
                for component in range(2):
                    value = source[
                        rank // 2, pl.ds(row, size), component * width : (component + 1) * width
                    ]
                    values.append(jnp.where(keep, value, 0.0))
                add_window(total, values, row, size, spot, width)

            for_rows(first, last, body)

        pl.when(active & (rank % 2 == depth))(functools.partial(put, kept))
        pl.when(active & (rank % 2 != depth))(functools.partial(put, got))


def last_kernel(
    slots, width, columns, positions, counts, positions_before, counts_before, near, down, up, result,
    total, semaphore,
):
    here = survey(positions, counts, slots, width, columns)[0]
    before = survey(positions_before, counts_before, slots, width, columns)[0]
    total[...] = near[...]
    jobs = [(s["stay"], down, s["down"], 0, s["size"], s) for s in before]
    jobs += [(s["move"], up, s["up"] - s["first"], s["first"], width, s) for s in here]
    for active, packed, start, first, last, spot in jobs:

        def body(row, size):
            rows = pl.ds(pl.multiple_of(start + row, 8), size)
            values = [packed[rows, c * width : (c + 1) * width] for c in range(2)]
            add_window(total, values, row, size, spot, width)

        pl.when(active)(functools.partial(for_rows, first, last, body))
    copy = pltpu.make_async_copy(total, result.at[0], semaphore)
    copy.start()
    copy.wait()


def call(kernel, sizes, inputs, outputs, specs, out_specs, scratch=(), flops=0):
    moved = sum(x.size * x.dtype.itemsize for x in list(inputs) + list(outputs))
    return pl.pallas_call(
        functools.partial(kernel, *sizes),
        out_shape=outputs,
        in_specs=specs,
        out_specs=out_specs,
        scratch_shapes=list(scratch),
        compiler_params=pltpu.CompilerParams(vmem_limit_bytes=40 << 20),
        cost_estimate=pl.CostEstimate(flops=flops, bytes_accessed=moved, transcendentals=0),
        name=kernel.__name__,
    )(*inputs)


def shards(objects, probe, measured, positions, counts):
    slots, width = measured.shape[:2]
    columns = objects.shape[3]
    sizes = (slots, width, columns)
    tables = jnp.asarray(tables_of(width))
    down_rows, up_rows = bounds(slots, width)
    f32 = jnp.float32
    down_shape = jax.ShapeDtypeStruct((down_rows, 2 * width), f32)
    up_shape = jax.ShapeDtypeStruct((up_rows, 2 * width), f32)
    level_shape = jax.ShapeDtypeStruct((slots // 2, width, width), f32)
    half_shape = jax.ShapeDtypeStruct((slots, width, 2 * width), f32)
    tile_shape = jax.ShapeDtypeStruct(objects.shape[1:], f32)

    here = (positions, counts)
    both = here + (shift(positions, "lat", 1), shift(counts, "lat", 1))
    up, levels = call(
        up_kernel, sizes, here + (objects, measured), [up_shape, level_shape],
        [SMEM] * 2 + [VMEM, ANY], [VMEM] * 2, [pltpu.SemaphoreType.DMA((slots // 2,))],
    )
    up = shift(up, "lat", 1)
    levels = shift(levels, "lat", 1)
    down = call(down_kernel, sizes, both[2:] + (objects,), [down_shape], [SMEM] * 2 + [VMEM], [VMEM])[0]
    down = shift(down, "lat", -1)
    own, given = call(
        local_kernel, sizes, both + (objects,), [half_shape] * 2, [SMEM] * 4 + [VMEM], [VMEM] * 2
    )
    got = shift(given, "depth", 1)
    up_other = shift(up, "depth", 1)
    down_other = shift(down, "depth", 1)
    kept, given = call(
        wave_kernel,
        sizes,
        both + (probe, measured, levels, own, got, down, down_other, up, up_other, tables),
        [half_shape] * 2,
        [SMEM] * 4 + [VMEM] * 10,
        [VMEM] * 2,
        [
            pltpu.VMEM((2, slots, width, 2 * width), f32),
            pltpu.VMEM((slots, width, width), f32),
            pltpu.SMEM((slots, 2), jnp.int32),
        ],
        slots // 2 * 4 * 2 * 12 * 2 * width**3,
    )
    got = shift(given, "depth", 1)
    down, up = call(
        spill_kernel, sizes, both + (kept, got), [down_shape, up_shape],
        [SMEM] * 4 + [VMEM] * 2, [VMEM] * 2,
    )
    down = shift(down, "lat", 1)
    up = shift(up, "lat", -1)
    near = call(
        near_kernel, sizes, both + (kept, got), [tile_shape], [SMEM] * 4 + [VMEM] * 2, [VMEM]
    )[0]
    return call(
        last_kernel, sizes, both + (near, down, up), [jax.ShapeDtypeStruct(objects.shape, f32)],
        [SMEM] * 4 + [VMEM] * 3, [ANY],
        [pltpu.VMEM(objects.shape[1:], f32), pltpu.SemaphoreType.DMA],
    )[0]


def solution(mesh):
    return jax.shard_map(
        shards,
        mesh=mesh,
        in_specs=(
            P("depth", None, "lat", None),
            P(),
            P("lat", None, None),
            P("lat", None),
            P("lat"),
        ),
        out_specs=P("depth", None, "lat", None),
        check_vma=False,
    )
```
